32 devices in a mesh: docs: 8 (over y, x, core), feat: 4 (over z).
Axes of the slice: x: 2, y: 2, z: 4, core: 2. Of those that a mesh axis runs over, the one named last changes fastest.
Arguments:
- feature_ids: int32 [2048, 512], P('docs', 'feat'), may hold values from 0 to 32767
- feature_weights: bfloat16 [2048, 512], P('docs', 'feat'), may hold values from 1 to 8
- projection: bfloat16 [131072, 256], P('feat'), may hold values from -6 to 6
- bucket_lists: int32 [2048, 32, 2], P('docs', 'feat'), may hold values from 0 to 4095, as said below
- bucket_counts: int32 [256, 4], P('docs', 'feat'), may hold values from 0 to 128, as said below
Outputs:
- cosine_tiles: float32 [256, 4, 128, 128], P('docs', 'feat')
- affinity: float32 [256, 4, 128], P('docs', 'feat')
The draws below stay inside these ranges and needn't reach their ends.
Inputs may be any that keep to these rules, and one draw needn't show every extreme that they name: bucket_lists[i, b] = (owner, slot): owner is an index of docs, slot a slot of that owner; bucket t is slots t * 128 to (t + 1) * 128 - 1. Within one band block, no two entries share owner and slot. The entries of one device (its documents times its band block) name one owner at most 512 times, and in every band block some owner is named 512 times by every device. bucket_counts[o * 32 + t, f] is the number of entries of band block f in bucket t of owner o; they fill exactly its first slots.
All inputs are finite; a program needn't handle non-finite values.
Results may differ from the reference program's by a relative error of at most 0.0007.
Values may be sent and summed in bfloat16 or wider, within the bound.
No kernel may reach another device: no remote copies, remote signals or barrier semaphores. Data moves between devices by JAX's collectives and lax.ppermute only.
A program may use at most 128 MiB of HBM per device.

```python
import math
import jax
import jax.numpy as jnp
import numpy as np
from jax import lax

SIG = 256
FEATURES = 131072
NNZ = 128
DOC_DEV = 256
BANDS = 32
TILE = 128
FBLK = 32768
NDOC = 2048
BAND_DEV = 8
CAP = 512
TILES = 32
N_DOCS = 8
N_FEAT = 4


def bucket_plan(key):
    plan_key = jax.random.fold_in(key, 4242)
    row_total = DOC_DEV * BAND_DEV
    positions = N_DOCS * CAP

    def one_block(block_key):
        key_hot, key_mult, key_send, key_own = jax.random.split(block_key, 4)
        hottest = jax.random.randint(key_hot, (), 0, N_DOCS)
        weights = jax.random.randint(key_mult, (N_DOCS,), 1, 5)
        target_owner = jnp.arange(positions) // CAP

        def one_sender(sender_key):
            key_score, key_perm = jax.random.split(sender_key)
            raw_score = jax.random.randint(key_score, (positions,), 0, 4096)
            rank_score = raw_score * weights[target_owner] + jnp.where(target_owner == hottest, 32768, 0)
            rank_score = rank_score * positions + jnp.arange(positions)
            unused, chosen = lax.top_k(rank_score, row_total)
            return chosen[jax.random.permutation(key_perm, row_total)]
        row_place = jax.vmap(one_sender)(jax.random.split(key_send, N_DOCS))
        sender_ids = jnp.arange(N_DOCS)[:, None]
        occupied = jnp.zeros((N_DOCS, positions), jnp.int32).at[sender_ids, row_place].set(1)
        incoming = occupied.reshape(N_DOCS, N_DOCS, CAP).transpose(1, 0, 2).reshape(N_DOCS, positions)

        def one_owner(owner_key, filled):
            key_order, key_shift = jax.random.split(owner_key)
            raw_order = jax.random.randint(key_order, (positions,), 0, 4096)
            order_score = (filled * 4096 + raw_order) * positions + jnp.arange(positions)
            ordering = jnp.argsort(-order_score)
            ranking = jnp.zeros((positions,), jnp.int32).at[ordering].set(jnp.arange(positions, dtype=jnp.int32))
            total_live = jnp.sum(filled)
            even_share = total_live // TILES + (jnp.arange(TILES) < total_live % TILES).astype(jnp.int32)
            first_half = even_share[0::2]
            second_half = even_share[1::2]
            lowest = jnp.maximum(-first_half, second_half - TILE)
            highest = jnp.minimum(TILE - first_half, second_half)
            shift_by = lowest + jax.random.randint(key_shift, (TILES // 2,), 0, 1 << 20) % (highest - lowest + 1)
            tile_sizes = jnp.stack([first_half + shift_by, second_half - shift_by], axis=1).reshape(TILES)
            tile_ends = jnp.cumsum(tile_sizes)
            tile_starts = tile_ends - tile_sizes
            tile_of = jnp.minimum(jnp.sum((ranking[:, None] >= tile_ends[None, :]).astype(jnp.int32), axis=1), TILES - 1)
            slot_of = tile_of * TILE + ranking - tile_starts[tile_of]
            return (slot_of, tile_sizes)
        slot_table, tile_sizes = jax.vmap(one_owner)(jax.random.split(key_own, N_DOCS), incoming)
        owner_of = row_place // CAP
        slot_rows = slot_table[owner_of, sender_ids * CAP + row_place % CAP]
        return (jnp.stack([owner_of, slot_rows], axis=-1), tile_sizes)
    plan_lists, tile_sizes = jax.vmap(one_block)(jax.random.split(plan_key, N_FEAT))
    plan_lists = plan_lists.reshape(N_FEAT, N_DOCS, DOC_DEV, BAND_DEV, 2).transpose(1, 2, 0, 3, 4)
    plan_lists = plan_lists.reshape(N_DOCS * DOC_DEV, BANDS, 2)
    tile_sizes = tile_sizes.transpose(1, 2, 0).reshape(N_DOCS * TILES, N_FEAT)
    return (plan_lists.astype(jnp.int32), tile_sizes.astype(jnp.int32))


def draw_bucket_lists(key, part):
    return bucket_plan(key)[0]


def draw_bucket_counts(key, part):
    return bucket_plan(key)[1]


def set_ends(array, own_key, smallest, high):
    shape = array.shape
    spot = [jax.random.randint(jax.random.fold_in(own_key, axis), (), 0, shape[axis]) for axis in range(len(shape))]
    array = array.at[tuple(spot)].set(smallest)
    longest = shape.index(max(shape))
    spot[longest] = (spot[longest] + 1) % shape[longest]
    return array.at[tuple(spot)].set(high)


def shard_levels(rng, extent, shards, smallest, high):
    def one(dim, parts):
        steps = jax.random.uniform(jax.random.fold_in(jax.random.fold_in(rng, 6), dim), (parts,), jnp.float32, smallest / len(shards), high / len(shards))
        return jnp.repeat(jnp.exp(steps), extent[dim] // parts).reshape((-1,) + (1,) * (len(extent) - dim - 1))

    factor_of = one(*shards[0])
    for cut in shards[1:]:
        factor_of = factor_of * one(*cut)
    return factor_of


def rank_bounds(number_of, skew):
    weights = [(1 << 20) // math.isqrt(rank ** skew) + 1 for rank in range(1, number_of + 1)]
    width = 1 + sum(weights) // (1 << 30)
    return np.cumsum(np.array([max(1, weight // width) for weight in weights]))


def ranked_ids(own_key, dims, count, skew):
    table = rank_bounds(count, skew)
    ticket = jax.random.randint(jax.random.fold_in(own_key, 1), dims, 0, int(table[count - 1]))
    grade = jnp.searchsorted(jnp.asarray(table, jnp.int32), ticket, side="right")
    return jax.random.permutation(jax.random.fold_in(own_key, 2), count)[grade].astype(jnp.int32)


def noise(own_key, dims, scale, limit, pieces=(), held_as=jnp.bfloat16):
    level = shard_levels(own_key, dims, pieces, -0.22, 0.18) if pieces else 1.0
    array = jax.random.normal(own_key, dims, jnp.float32) * scale * level
    return jnp.minimum(jnp.maximum(array, -limit), limit).astype(held_as)


def setup_inputs(seed: int = 0) -> dict:
    key_of = jax.random.split(jax.random.key(seed), 6)
    return {
        "feature_ids": set_ends(ranked_ids(key_of[0], (NDOC, N_FEAT * NNZ), FBLK, 2), jax.random.fold_in(key_of[0], 3), 0, FBLK - 1).astype(jnp.int32),
        "feature_weights": jnp.clip(jnp.exp(math.log(8.0) - 2.0794415 * jax.random.uniform(key_of[1], (NDOC, N_FEAT * NNZ), jnp.float32) ** shard_levels(key_of[1], (NDOC, N_FEAT * NNZ), ((0, 8), (1, 4)), -0.2, 0.2)), 1.0, 8.0).astype(jnp.bfloat16),
        "projection": noise(key_of[2], (FEATURES, SIG), 1.0, 6.0, ((0, 4),)),
        "bucket_lists": draw_bucket_lists(jax.random.fold_in(key_of[5], 71), 0),
        "bucket_counts": draw_bucket_counts(jax.random.fold_in(key_of[5], 71), 0),
    }


epsilon = 1e-06

def project_docs(ids_block, weight_block, projection, offsets):
    gathered = projection[ids_block + offsets[None, :]].astype(jnp.float32)
    return jnp.einsum('dn,dns->ds', weight_block.astype(jnp.float32), gathered)

def reference(feature_ids, feature_weights, projection, bucket_lists, bucket_counts):
    offsets = (jnp.arange(N_FEAT * NNZ) // NNZ * FBLK).astype(jnp.int32)
    doc_blocks = NDOC // 64
    id_blocks = feature_ids.reshape(doc_blocks, 64, N_FEAT * NNZ)
    weight_blocks = feature_weights.reshape(doc_blocks, 64, N_FEAT * NNZ)
    signature = lax.map(lambda pair: project_docs(pair[0], pair[1], projection, offsets), (id_blocks, weight_blocks))
    signature = signature.reshape(NDOC, SIG)
    unit_sig = (signature * lax.rsqrt(lax.optimization_barrier(jnp.sum(signature * signature, axis=1, keepdims=True)) + epsilon)).astype(jnp.bfloat16)
    room_size = TILES * TILE
    tiles_out = []
    affinity_out = []
    for feat_block in range(N_FEAT):
        bucket_table = jnp.zeros((N_DOCS * room_size, SIG), jnp.bfloat16)
        for band_step in range(BAND_DEV):
            column = bucket_lists[:, feat_block * BAND_DEV + band_step]
            target = (column[:, 0] * room_size + column[:, 1]).astype(jnp.int32)
            bucket_table = bucket_table.at[target].set(unit_sig)
        tile_rows = bucket_table.reshape(N_DOCS * TILES, TILE, SIG).astype(jnp.float32)
        products = jnp.einsum('tis,tjs->tij', tile_rows, tile_rows)
        filled = bucket_counts[:, feat_block]
        filled_mask = (jnp.arange(TILE)[None, :] < filled[:, None]).astype(jnp.float32)
        cosine = products * filled_mask[:, :, None] * filled_mask[:, None, :]
        self_term = jnp.diagonal(cosine, axis1=1, axis2=2)
        divisor = jnp.maximum(filled - 1, 1).astype(jnp.float32)
        tiles_out.append(cosine)
        affinity_out.append((lax.optimization_barrier(jnp.sum(cosine, axis=2)) - self_term) / divisor[:, None])
    return (jnp.stack(tiles_out, axis=1), jnp.stack(affinity_out, axis=1))
```

```python
import functools

import jax
import jax.numpy as jnp
from jax import lax
from jax.experimental import pallas as pl
from jax.experimental.pallas import tpu as pltpu
from jax.sharding import PartitionSpec as P

TILE = 128
LO = 128
EPSILON = 1e-06


def _fits(count, most):
    while count % most:
        most -= 1
    return most


def _signature_kernel(
    docs, entries, hi_n, stride, unroll, k_step, parts,
    ids_ref, w_ref, proj_ref, *rest,
):
    out_refs = rest[:parts]
    proj, counts, lhs, weights, total, sems = rest[parts:]
    chunks, chunk_rows, _ = proj.shape

    def chunk_copy(c):
        return pltpu.make_async_copy(
            proj_ref.at[pl.ds(c * chunk_rows, chunk_rows), :], proj.at[c], sems.at[c]
        )

    for c in range(chunks):
        chunk_copy(c).start()
    weights[...] = w_ref[...].astype(jnp.float32)

    def pair(p):
        iota_hi = lax.broadcasted_iota(jnp.int32, (hi_n, entries), 0).astype(jnp.bfloat16)
        iota_lo = lax.broadcasted_iota(jnp.int32, (LO, entries), 0).astype(jnp.bfloat16)
        one_hi = jnp.ones((hi_n, entries), jnp.bfloat16)
        zero_hi = jnp.zeros((hi_n, entries), jnp.bfloat16)
        zero_lo = jnp.zeros((LO, entries), jnp.bfloat16)
        his, los = [], []
        for e in range(2):
            ids = ids_ref[pl.ds(2 * p + e, 1), :]
            w = weights[pl.ds(2 * p + e, 1), :].astype(jnp.bfloat16)
            hi = (ids // LO).astype(jnp.float32).astype(jnp.bfloat16)
            lo = (ids % LO).astype(jnp.float32).astype(jnp.bfloat16)
            his.append(jnp.where(iota_hi == hi, one_hi, zero_hi))
            lo_w = jnp.where(iota_lo == lo, jnp.broadcast_to(w, (LO, entries)), zero_lo)
            los.append(jnp.concatenate([lo_w, zero_lo] if e == 0 else [zero_lo, lo_w], axis=1))
        r = lax.dot_general(
            jnp.concatenate(his, axis=1), jnp.concatenate(los, axis=0),
            (((1,), (1,)), ((), ())), preferred_element_type=jnp.float32,
        )
        for e in range(2):
            for t in range(hi_n // 8):
                counts[pl.ds(t * 8 * stride + 2 * p + e, 8, stride=stride), :] = r[
                    t * 8:(t + 1) * 8, e * LO:(e + 1) * LO
                ]

    def pairs(i, _):
        for u in range(unroll):
            pair(i * unroll + u)
        return 0

    lax.fori_loop(0, docs // 2 // unroll, pairs, 0)

    per_chunk = chunk_rows // LO
    for c in range(chunks):
        chunk_copy(c).wait()

        def multiply(k, _, c=c):
            for q in range(k_step):
                row = pl.multiple_of((c * per_chunk + k_step * k + q) * stride, 8)
                a = counts[pl.ds(row, docs), :]
                top = a.astype(jnp.bfloat16)
                lhs[:docs, q * LO:(q + 1) * LO] = top
                lhs[docs:, q * LO:(q + 1) * LO] = (a - top.astype(jnp.float32)).astype(jnp.bfloat16)
            first = pl.multiple_of(k * k_step * LO, k_step * LO)
            r = jnp.dot(
                lhs[...], proj[c, pl.ds(first, k_step * LO), :],
                preferred_element_type=jnp.float32,
            )
            r = r[:docs] + r[docs:]
            if c == 0:
                total[...] = jnp.where(k == 0, r, total[...] + r)
            else:
                total[...] += r
            return 0

        lax.fori_loop(0, per_chunk // k_step, multiply, 0)

    part_rows = docs // parts
    me = lax.axis_index("feat")
    for k in range(parts):
        row = pl.multiple_of((me ^ k) * part_rows, part_rows)
        out_refs[k][...] = total[pl.ds(row, part_rows), :]


def _signature_parts(ids, w, projection, parts):
    docs, entries = ids.shape
    feats, width = projection.shape
    hi_n = feats // LO
    chunks = 4
    stride = docs + 8
    k_step = _fits(hi_n // chunks, 32)
    unroll = _fits(docs // 2, 16)
    return pl.pallas_call(
        functools.partial(
            _signature_kernel, docs, entries, hi_n, stride, unroll, k_step, parts
        ),
        out_shape=[jax.ShapeDtypeStruct((docs // parts, width), jnp.float32)] * parts,
        in_specs=[
            pl.BlockSpec(memory_space=pltpu.VMEM),
            pl.BlockSpec(memory_space=pltpu.VMEM),
            pl.BlockSpec(memory_space=pl.ANY),
        ],
        out_specs=[pl.BlockSpec(memory_space=pltpu.VMEM)] * parts,
        scratch_shapes=[
            pltpu.VMEM((chunks, feats // chunks, width), jnp.bfloat16),
            pltpu.VMEM((hi_n * stride, LO), jnp.float32),
            pltpu.VMEM((2 * docs, k_step * LO), jnp.bfloat16),
            pltpu.VMEM((docs, entries), jnp.float32),
            pltpu.VMEM((docs, width), jnp.float32),
            pltpu.SemaphoreType.DMA((chunks,)),
        ],
        compiler_params=pltpu.CompilerParams(vmem_limit_bytes=60 << 20),
    )(ids, w, projection)


def _unit_kernel(*refs):
    total = refs[0][...]
    for ref in refs[1:-1]:
        total = total + ref[...]
    scale = lax.rsqrt(jnp.sum(total * total, axis=1, keepdims=True) + EPSILON)
    refs[-1][...] = (total * scale).astype(jnp.bfloat16)


def _unit(parts):
    return pl.pallas_call(
        _unit_kernel,
        out_shape=jax.ShapeDtypeStruct(parts[0].shape, jnp.bfloat16),
        in_specs=[pl.BlockSpec(memory_space=pltpu.VMEM)] * len(parts),
        out_specs=pl.BlockSpec(memory_space=pltpu.VMEM),
    )(*parts)


def _source_kernel(docs, tiles, rows_dev, shard, targets_ref, out_ref):
    me_docs = lax.axis_index("docs")
    me_feat = lax.axis_index("feat")
    sub = docs // 128
    base = me_docs * (tiles * TILE)
    iota_lo = lax.broadcasted_iota(jnp.int32, (TILE, 128), 0).astype(jnp.bfloat16)
    iota_hi = lax.broadcasted_iota(jnp.int32, (tiles, 128), 0).astype(jnp.bfloat16)
    one_lo = jnp.ones((TILE, 128), jnp.bfloat16)
    zero_lo = jnp.zeros((TILE, 128), jnp.bfloat16)
    zero_hi = jnp.zeros((tiles, 128), jnp.bfloat16)
    lane = lax.broadcasted_iota(jnp.int32, (1, 128), 1)
    out_ref[...] = jnp.zeros_like(out_ref)

    def step(i, _):
        block = targets_ref[pl.ds(pl.multiple_of(i * 8, 8), 8), :] - base
        dev = ((i * 8) // rows_dev) ^ me_docs
        dev_row = jnp.full((tiles, 128), dev.astype(jnp.float32), jnp.float32).astype(jnp.bfloat16)
        los, his = [], []
        for r in range(8):
            row = block[r:r + 1, :]
            hi = (row >> 7).astype(jnp.float32).astype(jnp.bfloat16)
            lo = (row & 127).astype(jnp.float32).astype(jnp.bfloat16)
            place = ((r % sub) * 128 + lane) ^ (me_feat * shard)
            place = place.astype(jnp.float32).astype(jnp.bfloat16)
            los.append(jnp.where(iota_lo == lo, one_lo, zero_lo))
            here = iota_hi == hi
            his.append(jnp.concatenate([
                jnp.where(here, jnp.broadcast_to(place, (tiles, 128)), zero_hi),
                jnp.where(here, dev_row, zero_hi),
            ], axis=0))
        out_ref[...] += lax.dot_general(
            jnp.concatenate(los, axis=1), jnp.concatenate(his, axis=1),
            (((1,), (1,)), ((), ())), preferred_element_type=jnp.float32,
        )
        return 0

    lax.fori_loop(0, targets_ref.shape[0] // 8, step, 0)


def _sources(targets, docs, tiles, rows_dev, shard):
    return pl.pallas_call(
        functools.partial(_source_kernel, docs, tiles, rows_dev, shard),
        out_shape=jax.ShapeDtypeStruct((TILE, 2 * tiles), jnp.float32),
        in_specs=[pl.BlockSpec(memory_space=pltpu.VMEM)],
        out_specs=pl.BlockSpec(memory_space=pltpu.VMEM),
    )(targets)


def _tiles_kernel(blocks, group, counts_ref, source_ref, *rest):
    unit_refs = rest[:blocks]
    cosine_hbm, affinity_ref, cosine, sems = rest[blocks:]
    tiles = cosine.shape[0]
    docs = unit_refs[0].shape[0]
    lane = lax.broadcasted_iota(jnp.int32, (TILE, docs), 1).astype(jnp.bfloat16)
    one = jnp.ones((TILE, docs), jnp.bfloat16)
    zero = jnp.zeros((TILE, docs), jnp.bfloat16)
    row_of = lax.broadcasted_iota(jnp.int32, (TILE, TILE), 0)
    col_of = lax.broadcasted_iota(jnp.int32, (TILE, TILE), 1)
    place = source_ref[:, :tiles] + source_ref[:, tiles:] * docs

    def copy_out(g):
        span = pl.ds(g * group, group)
        return pltpu.make_async_copy(cosine.at[span], cosine_hbm.at[span], sems.at[g])

    for g in range(tiles // group):
        total = jnp.zeros((group * TILE, unit_refs[0].shape[1]), jnp.float32)
        sources = [
            jnp.broadcast_to(place[:, t:t + 1], (TILE, docs))
            for t in range(g * group, (g + 1) * group)
        ]
        for b in range(blocks):
            pick = jnp.concatenate([
                jnp.where(lane == (s - b * docs).astype(jnp.bfloat16), one, zero) for s in sources
            ], axis=0)
            total = total + jnp.dot(pick, unit_refs[b][...], preferred_element_type=jnp.float32)
        table = total.astype(jnp.bfloat16)
        for j in range(group):
            t = g * group + j
            rows = table[j * TILE:(j + 1) * TILE]
            filled = counts_ref[t, 0]
            products = lax.dot_general(
                rows, rows, (((1,), (1,)), ((), ())), preferred_element_type=jnp.float32
            )
            products = jnp.where(jnp.maximum(row_of, col_of) < filled, products, 0.0)
            cosine[t] = products
            others = jnp.sum(jnp.where(row_of == col_of, 0.0, products), axis=0, keepdims=True)
            divisor = jnp.full((1, TILE), jnp.maximum(filled - 1, 1).astype(jnp.float32))
            affinity_ref[t:t + 1, :] = others / divisor
        copy_out(g).start()
    for g in range(tiles // group):
        copy_out(g).wait()


def _tiles(counts, source, units):
    tiles = counts.shape[0]
    group = _fits(tiles, 4)
    return pl.pallas_call(
        functools.partial(_tiles_kernel, len(units), group),
        out_shape=[
            jax.ShapeDtypeStruct((tiles, TILE, TILE), jnp.float32),
            jax.ShapeDtypeStruct((tiles, TILE), jnp.float32),
        ],
        in_specs=[pl.BlockSpec(memory_space=pltpu.SMEM)]
        + [pl.BlockSpec(memory_space=pltpu.VMEM)] * (1 + len(units)),
        out_specs=[pl.BlockSpec(memory_space=pl.ANY), pl.BlockSpec(memory_space=pltpu.VMEM)],
        scratch_shapes=[
            pltpu.VMEM((tiles, TILE, TILE), jnp.float32),
            pltpu.SemaphoreType.DMA((tiles // group,)),
        ],
        compiler_params=pltpu.CompilerParams(vmem_limit_bytes=48 << 20),
    )(counts, source, *units)


def solution(mesh):
    n_docs, n_feat = mesh.shape["docs"], mesh.shape["feat"]

    def send(x, axis, size, k):
        return lax.ppermute(x, axis, [(i, i ^ k) for i in range(size)])

    def per_device(ids, w, projection, lists, counts):
        docs = ids.shape[0]
        tiles = counts.shape[0]
        shard = docs // n_feat
        targets = (lists[:, :, 0] * (tiles * TILE) + lists[:, :, 1]).T.reshape(-1, 128)
        rows_dev = targets.shape[0]
        targets = lax.all_gather(targets, "docs", axis=0, tiled=True)
        parts = _signature_parts(ids, w, projection, n_feat)
        received = [send(parts[k], "feat", n_feat, k) for k in range(1, n_feat)]
        source = _sources(targets, docs, tiles, rows_dev, shard)
        own = _unit([parts[0]] + received)
        own = jnp.concatenate([own] + [send(own, "feat", n_feat, k) for k in range(1, n_feat)])
        near = [own] + [send(own, "docs", n_docs, k) for k in range(2, n_docs, 2)]
        units = []
        for block in near:
            units += [block, send(block, "docs", n_docs, 1)]
        cosine, affinity = _tiles(counts, source, units)
        return cosine[:, None], affinity[:, None]

    placed = (
        P("docs", "feat"),
        P("docs", "feat"),
        P("feat", None),
        P("docs", "feat", None),
        P("docs", "feat"),
    )
    return jax.shard_map(
        per_device,
        mesh=mesh,
        in_specs=placed,
        out_specs=(P("docs", "feat", None, None), P("docs", "feat", None)),
        check_vma=False,
    )
```

```python
import functools

import jax
import jax.numpy as jnp
from jax import lax
from jax.experimental import pallas as pl
from jax.experimental.pallas import tpu as pltpu
from jax.sharding import PartitionSpec as P

TILE = 128
LO = 128
EPSILON = 1e-06
VMEM_SMALL = 8 << 20
VMEM_SIGNATURE = 60 << 20
VMEM_TILES = 24 << 20


def _fits(count, most):
    while count % most:
        most -= 1
    return most


def _signature_kernel(
    first, docs, entries, hi_n, stride, unroll, k_step, parts,
    ids_ref, w_ref, proj_ref, *rest,
):
    out_refs = rest[:parts]
    proj, counts, lhs, weights, total, sems = rest[parts:]
    chunks, chunk_rows, _ = proj.shape

    def chunk_copy(c):
        return pltpu.make_async_copy(
            proj_ref.at[pl.ds(c * chunk_rows, chunk_rows), :], proj.at[c], sems.at[c]
        )

    for c in range(chunks):
        chunk_copy(c).start()
    weights[...] = w_ref[first:first + docs, :].astype(jnp.float32)

    def pair(p):
        iota_hi = lax.broadcasted_iota(jnp.int32, (hi_n, entries), 0).astype(jnp.bfloat16)
        iota_lo = lax.broadcasted_iota(jnp.int32, (LO, entries), 0).astype(jnp.bfloat16)
        one_hi = jnp.ones((hi_n, entries), jnp.bfloat16)
        zero_hi = jnp.zeros((hi_n, entries), jnp.bfloat16)
        zero_lo = jnp.zeros((LO, entries), jnp.bfloat16)
        his, los = [], []
        for e in range(2):
            ids = ids_ref[pl.ds(first + 2 * p + e, 1), :]
            w = weights[pl.ds(2 * p + e, 1), :].astype(jnp.bfloat16)
            hi = (ids // LO).astype(jnp.float32).astype(jnp.bfloat16)
            lo = (ids % LO).astype(jnp.float32).astype(jnp.bfloat16)
            his.append(jnp.where(iota_hi == hi, one_hi, zero_hi))
            lo_w = jnp.where(iota_lo == lo, jnp.broadcast_to(w, (LO, entries)), zero_lo)
            los.append(jnp.concatenate([lo_w, zero_lo] if e == 0 else [zero_lo, lo_w], axis=1))
        r = lax.dot_general(
            jnp.concatenate(his, axis=1), jnp.concatenate(los, axis=0),
            (((1,), (1,)), ((), ())), preferred_element_type=jnp.float32,
        )
        for e in range(2):
            for t in range(hi_n // 8):
                counts[pl.ds(t * 8 * stride + 2 * p + e, 8, stride=stride), :] = r[
                    t * 8:(t + 1) * 8, e * LO:(e + 1) * LO
                ]

    def pairs(i, _):
        for u in range(unroll):
            pair(i * unroll + u)
        return 0

    lax.fori_loop(0, docs // 2 // unroll, pairs, 0)

    per_chunk = chunk_rows // LO
    for c in range(chunks):
        chunk_copy(c).wait()

        def multiply(k, _, c=c):
            for q in range(k_step):
                row = pl.multiple_of((c * per_chunk + k_step * k + q) * stride, 8)
                a = counts[pl.ds(row, docs), :]
                top = a.astype(jnp.bfloat16)
                lhs[:docs, q * LO:(q + 1) * LO] = top
                lhs[docs:, q * LO:(q + 1) * LO] = (a - top.astype(jnp.float32)).astype(jnp.bfloat16)
            feature = pl.multiple_of(k * k_step * LO, k_step * LO)
            r = jnp.dot(
                lhs[...], proj[c, pl.ds(feature, k_step * LO), :],
                preferred_element_type=jnp.float32,
            )
            r = r[:docs] + r[docs:]
            if c == 0:
                total[...] = jnp.where(k == 0, r, total[...] + r)
            else:
                total[...] += r
            return 0

        lax.fori_loop(0, per_chunk // k_step, multiply, 0)

    part_rows = docs // parts
    me = lax.axis_index("feat")
    for k in range(parts):
        row = pl.multiple_of((me ^ k) * part_rows, part_rows)
        out_refs[k][...] = total[pl.ds(row, part_rows), :]


def _signature_parts(ids, w, projection, parts, first, docs):
    entries = ids.shape[1]
    feats, width = projection.shape
    hi_n = feats // LO
    chunks = 2
    stride = docs + 8
    k_step = _fits(hi_n // chunks, 64)
    unroll = _fits(docs // 2, 64)
    return pl.pallas_call(
        functools.partial(
            _signature_kernel, first, docs, entries, hi_n, stride, unroll, k_step, parts
        ),
        out_shape=[jax.ShapeDtypeStruct((docs // parts, width), jnp.float32)] * parts,
        in_specs=[
            pl.BlockSpec(memory_space=pltpu.VMEM),
            pl.BlockSpec(memory_space=pltpu.VMEM),
            pl.BlockSpec(memory_space=pl.ANY),
        ],
        out_specs=[pl.BlockSpec(memory_space=pltpu.VMEM)] * parts,
        scratch_shapes=[
            pltpu.VMEM((chunks, feats // chunks, width), jnp.bfloat16),
            pltpu.VMEM((hi_n * stride, LO), jnp.float32),
            pltpu.VMEM((2 * docs, k_step * LO), jnp.bfloat16),
            pltpu.VMEM((docs, entries), jnp.float32),
            pltpu.VMEM((docs, width), jnp.float32),
            pltpu.SemaphoreType.DMA((chunks,)),
        ],
        compiler_params=pltpu.CompilerParams(vmem_limit_bytes=VMEM_SIGNATURE),
        cost_estimate=pl.CostEstimate(
            flops=6 * docs * feats * width, bytes_accessed=2 * feats * width, transcendentals=0
        ),
    )(ids, w, projection)


def _unit_kernel(*refs):
    total = refs[0][...]
    for ref in refs[1:-1]:
        total = total + ref[...]
    scale = lax.rsqrt(jnp.sum(total * total, axis=1, keepdims=True) + EPSILON)
    refs[-1][...] = (total * scale).astype(jnp.bfloat16)


def _unit(parts):
    return pl.pallas_call(
        _unit_kernel,
        out_shape=jax.ShapeDtypeStruct(parts[0].shape, jnp.bfloat16),
        in_specs=[pl.BlockSpec(memory_space=pltpu.VMEM)] * len(parts),
        out_specs=pl.BlockSpec(memory_space=pltpu.VMEM),
        compiler_params=pltpu.CompilerParams(vmem_limit_bytes=VMEM_SMALL),
    )(*parts)


def _source_kernel(docs, tiles, rows_dev, shard, targets_ref, out_ref, sums):
    me_docs = lax.axis_index("docs")
    me_feat = lax.axis_index("feat")
    sub = docs // 128
    base = me_docs * (tiles * TILE)
    iota_lo = lax.broadcasted_iota(jnp.int32, (TILE, 128), 0).astype(jnp.bfloat16)
    iota_hi = lax.broadcasted_iota(jnp.int32, (tiles, 128), 0).astype(jnp.bfloat16)
    one_lo = jnp.ones((TILE, 128), jnp.bfloat16)
    zero_lo = jnp.zeros((TILE, 128), jnp.bfloat16)
    zero_hi = jnp.zeros((tiles, 128), jnp.bfloat16)
    lane = lax.broadcasted_iota(jnp.int32, (1, 128), 1)
    sums[...] = jnp.zeros_like(sums)

    def step(i, _):
        block = targets_ref[pl.ds(pl.multiple_of(i * 8, 8), 8), :].astype(jnp.int32) - base
        dev = (i * 8) // rows_dev
        dev_row = jnp.full((tiles, 128), dev.astype(jnp.float32), jnp.float32).astype(jnp.bfloat16)
        los, his = [], []
        for r in range(8):
            row = block[r:r + 1, :]
            hi = (row >> 7).astype(jnp.float32).astype(jnp.bfloat16)
            lo = (row & 127).astype(jnp.float32).astype(jnp.bfloat16)
            place = ((r % sub) * 128 + lane) ^ (me_feat * shard)
            place = place.astype(jnp.float32).astype(jnp.bfloat16)
            los.append(jnp.where(iota_lo == lo, one_lo, zero_lo))
            here = iota_hi == hi
            his.append(jnp.concatenate([
                jnp.where(here, jnp.broadcast_to(place, (tiles, 128)), zero_hi),
                jnp.where(here, dev_row, zero_hi),
            ], axis=0))
        sums[...] += lax.dot_general(
            jnp.concatenate(los, axis=1), jnp.concatenate(his, axis=1),
            (((1,), (1,)), ((), ())), preferred_element_type=jnp.float32,
        )
        return 0

    lax.fori_loop(0, targets_ref.shape[0] // 8, step, 0)
    out_ref[...] = sums[:, :tiles] + sums[:, tiles:] * docs


def _sources(targets, docs, tiles, rows_dev, shard):
    return pl.pallas_call(
        functools.partial(_source_kernel, docs, tiles, rows_dev, shard),
        out_shape=jax.ShapeDtypeStruct((TILE, tiles), jnp.float32),
        in_specs=[pl.BlockSpec(memory_space=pltpu.VMEM)],
        out_specs=pl.BlockSpec(memory_space=pltpu.VMEM),
        scratch_shapes=[pltpu.VMEM((TILE, 2 * tiles), jnp.float32)],
        compiler_params=pltpu.CompilerParams(vmem_limit_bytes=VMEM_SMALL),
        cost_estimate=pl.CostEstimate(
            flops=2 * targets.size * TILE * TILE, bytes_accessed=4 * targets.size, transcendentals=0
        ),
    )(targets)


def _choose(pick, source_ref, tiles, blocks, rows, period, offset):
    lane = lax.broadcasted_iota(jnp.int32, (TILE, rows), 1).astype(jnp.bfloat16)
    one = jnp.ones((TILE, rows), jnp.bfloat16)
    zero = jnp.zeros((TILE, rows), jnp.bfloat16)
    for j, t in enumerate(tiles):
        s = jnp.broadcast_to(source_ref[:, t:t + 1], (TILE, rows))
        for b in range(blocks):
            here = (s - (b * period + offset)).astype(jnp.bfloat16)
            pick[j * TILE:(j + 1) * TILE, b * rows:(b + 1) * rows] = jnp.where(lane == here, one, zero)


def _collect(units, unit_refs):
    rows = unit_refs[0].shape[0]
    for b, ref in enumerate(unit_refs):
        units[b * rows:(b + 1) * rows, :] = ref[...]


def _place_kernel(blocks, group, period, offset, source_ref, *rest):
    unit_refs = rest[:blocks]
    table, units, pick = rest[blocks:]
    rows = unit_refs[0].shape[0]
    _collect(units, unit_refs)
    groups = table.shape[0] // (group * TILE)
    for g in range(-1, groups):
        if g + 1 < groups:
            span = range((g + 1) * group, (g + 2) * group)
            _choose(pick.at[(g + 1) % 2], source_ref, span, blocks, rows, period, offset)
        if g >= 0:
            table[g * group * TILE:(g + 1) * group * TILE, :] = jnp.dot(
                pick[g % 2], units[...], preferred_element_type=jnp.float32
            ).astype(jnp.bfloat16)


def _place(source, units, period, offset):
    tiles = source.shape[1]
    group = _fits(tiles, 4)
    rows, width = units[0].shape
    return pl.pallas_call(
        functools.partial(_place_kernel, len(units), group, period, offset),
        out_shape=jax.ShapeDtypeStruct((tiles * TILE, width), jnp.bfloat16),
        in_specs=[pl.BlockSpec(memory_space=pltpu.VMEM)] * (1 + len(units)),
        out_specs=pl.BlockSpec(memory_space=pltpu.VMEM),
        scratch_shapes=[
            pltpu.VMEM((len(units) * rows, width), jnp.bfloat16),
            pltpu.VMEM((2, group * TILE, len(units) * rows), jnp.bfloat16),
        ],
        compiler_params=pltpu.CompilerParams(vmem_limit_bytes=VMEM_TILES),
        cost_estimate=pl.CostEstimate(
            flops=2 * tiles * TILE * width * len(units) * rows,
            bytes_accessed=2 * tiles * TILE * width, transcendentals=0,
        ),
    )(source, *units)


def _tiles_kernel(blocks, group, period, offset, has_placed, counts_ref, source_ref, *rest):
    unit_refs = rest[:blocks]
    placed_ref = rest[blocks] if has_placed else None
    cosine_hbm, affinity_ref, cosine, units, pick, table, sems = rest[blocks + has_placed:]
    tiles = cosine.shape[0]
    rows = unit_refs[0].shape[0]
    row_of = lax.broadcasted_iota(jnp.int32, (TILE, TILE), 0)
    col_of = lax.broadcasted_iota(jnp.int32, (TILE, TILE), 1)
    _collect(units, unit_refs)

    def copy_out(g):
        span = pl.ds(g * group, group)
        return pltpu.make_async_copy(cosine.at[span], cosine_hbm.at[span], sems.at[g])

    def place(g):
        span = slice(g * group * TILE, (g + 1) * group * TILE)
        new = jnp.dot(pick[g % 2], units[...], preferred_element_type=jnp.float32).astype(jnp.bfloat16)
        table[span, :] = new + placed_ref[span, :] if has_placed else new

    def multiply(g):
        for t in range(g * group, (g + 1) * group):
            slots = table[t * TILE:(t + 1) * TILE, :]
            filled = counts_ref[t, 0]
            products = lax.dot_general(
                slots, slots, (((1,), (1,)), ((), ())), preferred_element_type=jnp.float32
            )
            products = jnp.where(jnp.maximum(row_of, col_of) < filled, products, 0.0)
            cosine[t] = products
            others = jnp.sum(jnp.where(row_of == col_of, 0.0, products), axis=0, keepdims=True)
            divisor = jnp.full((1, TILE), jnp.maximum(filled - 1, 1).astype(jnp.float32))
            affinity_ref[t:t + 1, :] = others / divisor
        copy_out(g).start()

    groups = tiles // group
    for g in range(-1, groups + 1):
        if g + 1 < groups:
            span = range((g + 1) * group, (g + 2) * group)
            _choose(pick.at[(g + 1) % 2], source_ref, span, blocks, rows, period, offset)
        if 0 <= g < groups:
            place(g)
        if g >= 1:
            multiply(g - 1)
    for g in range(groups):
        copy_out(g).wait()


def _tiles(counts, source, units, placed, period, offset):
    tiles = counts.shape[0]
    group = _fits(tiles, 4)
    rows, width = units[0].shape
    extra = [] if placed is None else [placed]
    return pl.pallas_call(
        functools.partial(_tiles_kernel, len(units), group, period, offset, len(extra)),
        out_shape=[
            jax.ShapeDtypeStruct((tiles, TILE, TILE), jnp.float32),
            jax.ShapeDtypeStruct((tiles, TILE), jnp.float32),
        ],
        in_specs=[pl.BlockSpec(memory_space=pltpu.SMEM)]
        + [pl.BlockSpec(memory_space=pltpu.VMEM)] * (1 + len(units) + len(extra)),
        out_specs=[pl.BlockSpec(memory_space=pl.ANY), pl.BlockSpec(memory_space=pltpu.VMEM)],
        scratch_shapes=[
            pltpu.VMEM((tiles, TILE, TILE), jnp.float32),
            pltpu.VMEM((len(units) * rows, width), jnp.bfloat16),
            pltpu.VMEM((2, group * TILE, len(units) * rows), jnp.bfloat16),
            pltpu.VMEM((tiles * TILE, width), jnp.bfloat16),
            pltpu.SemaphoreType.DMA((tiles // group,)),
        ],
        compiler_params=pltpu.CompilerParams(vmem_limit_bytes=VMEM_TILES),
        cost_estimate=pl.CostEstimate(
            flops=2 * tiles * TILE * width * (len(units) * rows + TILE),
            bytes_accessed=4 * tiles * TILE * TILE, transcendentals=0,
        ),
    )(counts, source, *units, *extra)


def solution(mesh):
    n_docs, n_feat = mesh.shape["docs"], mesh.shape["feat"]

    def send(x, axis, size, k):
        return lax.ppermute(x, axis, [(i, i ^ k) for i in range(size)])

    def everywhere(x, axis, size, step):
        return [x] + [send(x, axis, size, k) for k in range(step, size, step)]

    def per_device(ids, w, projection, lists, counts):
        docs = ids.shape[0]
        tiles = counts.shape[0]
        shard = docs // n_feat

        def targets_of(block):
            return (block[:, :, 0] * (tiles * TILE) + block[:, :, 1]).T.reshape(-1, 128)

        near = everywhere(targets_of(lists), "docs", n_docs, 2)
        own = _signature_parts(ids, w, projection, n_feat, 0, docs)
        near, own = lax.optimization_barrier((near, own))
        received = [send(own[k], "feat", n_feat, k) for k in range(1, n_feat)]
        near = jnp.stack(near)
        rows_dev = near.shape[1]
        targets = jnp.stack([near, send(near, "docs", n_docs, 1)], axis=1).reshape(-1, 128)
        source = _sources(targets, docs, tiles, rows_dev, shard)
        terms = [own[0] + received[0]] + received[1:]
        terms, source = lax.optimization_barrier((terms, source))
        unit = jnp.concatenate(everywhere(_unit(terms), "feat", n_feat, 1))
        near = everywhere(unit, "docs", n_docs, 2)
        units = [u for x in near for u in (x, send(x, "docs", n_docs, 1))]
        placed = _place(source, units[:2], docs, 0)
        cosine, affinity = _tiles(counts, source, units[2:], placed, docs, 2 * docs)
        return cosine[:, None], affinity[:, None]

    placed = (
        P("docs", "feat"),
        P("docs", "feat"),
        P("feat", None),
        P("docs", "feat", None),
        P("docs", "feat"),
    )
    return jax.shard_map(
        per_device,
        mesh=mesh,
        in_specs=placed,
        out_specs=(P("docs", "feat", None, None), P("docs", "feat", None)),
        check_vma=False,
    )
```

```python
import functools

import jax
import jax.numpy as jnp
from jax import lax
from jax.experimental import pallas as pl
from jax.experimental.pallas import tpu as pltpu
from jax.sharding import PartitionSpec as P

TILE = 128
LO = 128
EPSILON = 1e-06
VMEM_SMALL = 8 << 20
VMEM_SIGNATURE = 60 << 20
VMEM_TILES = 24 << 20


def _fits(count, most):
    while count % most:
        most -= 1
    return most


def _signature_kernel(
    first, docs, entries, hi_n, stride, unroll, k_step, parts,
    ids_ref, w_ref, proj_ref, *rest,
):
    out_refs = rest[:parts]
    proj, counts, lhs, weights, total, sems = rest[parts:]
    chunks, chunk_rows, _ = proj.shape

    def chunk_copy(c):
        return pltpu.make_async_copy(
            proj_ref.at[pl.ds(c * chunk_rows, chunk_rows), :], proj.at[c], sems.at[c]
        )

    for c in range(chunks):
        chunk_copy(c).start()
    weights[...] = w_ref[first:first + docs, :].astype(jnp.float32)

    def pair(p):
        iota_hi = lax.broadcasted_iota(jnp.int32, (hi_n, entries), 0).astype(jnp.bfloat16)
        iota_lo = lax.broadcasted_iota(jnp.int32, (LO, entries), 0).astype(jnp.bfloat16)
        one_hi = jnp.ones((hi_n, entries), jnp.bfloat16)
        zero_hi = jnp.zeros((hi_n, entries), jnp.bfloat16)
        zero_lo = jnp.zeros((LO, entries), jnp.bfloat16)
        his, los = [], []
        for e in range(2):
            ids = ids_ref[pl.ds(first + 2 * p + e, 1), :]
            w = weights[pl.ds(2 * p + e, 1), :].astype(jnp.bfloat16)
            hi = (ids // LO).astype(jnp.float32).astype(jnp.bfloat16)
            lo = (ids % LO).astype(jnp.float32).astype(jnp.bfloat16)
            his.append(jnp.where(iota_hi == hi, one_hi, zero_hi))
            lo_w = jnp.where(iota_lo == lo, jnp.broadcast_to(w, (LO, entries)), zero_lo)
            los.append(jnp.concatenate([lo_w, zero_lo] if e == 0 else [zero_lo, lo_w], axis=1))
        r = lax.dot_general(
            jnp.concatenate(his, axis=1), jnp.concatenate(los, axis=0),
            (((1,), (1,)), ((), ())), preferred_element_type=jnp.float32,
        )
        for e in range(2):
            for t in range(hi_n // 8):
                counts[pl.ds(t * 8 * stride + 2 * p + e, 8, stride=stride), :] = r[
                    t * 8:(t + 1) * 8, e * LO:(e + 1) * LO
                ]

    def pairs(i, _):
        for u in range(unroll):
            pair(i * unroll + u)
        return 0

    lax.fori_loop(0, docs // 2 // unroll, pairs, 0)

    per_chunk = chunk_rows // LO
    for c in range(chunks):
        chunk_copy(c).wait()

        def multiply(k, _, c=c):
            for q in range(k_step):
                row = pl.multiple_of((c * per_chunk + k_step * k + q) * stride, 8)
                a = counts[pl.ds(row, docs), :]
                top = a.astype(jnp.bfloat16)
                lhs[:docs, q * LO:(q + 1) * LO] = top
                lhs[docs:, q * LO:(q + 1) * LO] = (a - top.astype(jnp.float32)).astype(jnp.bfloat16)
            feature = pl.multiple_of(k * k_step * LO, k_step * LO)
            r = jnp.dot(
                lhs[...], proj[c, pl.ds(feature, k_step * LO), :],
                preferred_element_type=jnp.float32,
            )
            r = r[:docs] + r[docs:]
            if c == 0:
                total[...] = jnp.where(k == 0, r, total[...] + r)
            else:
                total[...] += r
            return 0

        lax.fori_loop(0, per_chunk // k_step, multiply, 0)

    part_rows = docs // parts
    me = lax.axis_index("feat")
    for k in range(parts):
        row = pl.multiple_of((me ^ k) * part_rows, part_rows)
        out_refs[k][...] = total[pl.ds(row, part_rows), :]


def _signature_parts(ids, w, projection, parts, first, docs):
    entries = ids.shape[1]
    feats, width = projection.shape
    hi_n = feats // LO
    chunks = 2
    stride = docs + 8
    k_step = _fits(hi_n // chunks, 64)
    unroll = _fits(docs // 2, 64)
    return pl.pallas_call(
        functools.partial(
            _signature_kernel, first, docs, entries, hi_n, stride, unroll, k_step, parts
        ),
        out_shape=[jax.ShapeDtypeStruct((docs // parts, width), jnp.float32)] * parts,
        in_specs=[
            pl.BlockSpec(memory_space=pltpu.VMEM),
            pl.BlockSpec(memory_space=pltpu.VMEM),
            pl.BlockSpec(memory_space=pl.ANY),
        ],
        out_specs=[pl.BlockSpec(memory_space=pltpu.VMEM)] * parts,
        scratch_shapes=[
            pltpu.VMEM((chunks, feats // chunks, width), jnp.bfloat16),
            pltpu.VMEM((hi_n * stride, LO), jnp.float32),
            pltpu.VMEM((2 * docs, k_step * LO), jnp.bfloat16),
            pltpu.VMEM((docs, entries), jnp.float32),
            pltpu.VMEM((docs, width), jnp.float32),
            pltpu.SemaphoreType.DMA((chunks,)),
        ],
        compiler_params=pltpu.CompilerParams(vmem_limit_bytes=VMEM_SIGNATURE),
        cost_estimate=pl.CostEstimate(
            flops=6 * docs * feats * width, bytes_accessed=2 * feats * width, transcendentals=0
        ),
    )(ids, w, projection)


def _unit_kernel(*refs):
    total = refs[0][...]
    for ref in refs[1:-1]:
        total = total + ref[...]
    scale = lax.rsqrt(jnp.sum(total * total, axis=1, keepdims=True) + EPSILON)
    refs[-1][...] = (total * scale).astype(jnp.bfloat16)


def _unit(parts):
    return pl.pallas_call(
        _unit_kernel,
        out_shape=jax.ShapeDtypeStruct(parts[0].shape, jnp.bfloat16),
        in_specs=[pl.BlockSpec(memory_space=pltpu.VMEM)] * len(parts),
        out_specs=pl.BlockSpec(memory_space=pltpu.VMEM),
        compiler_params=pltpu.CompilerParams(vmem_limit_bytes=VMEM_SMALL),
    )(*parts)


def _source_kernel(docs, tiles, rows_dev, shard, step_rows, targets_ref, out_ref, sums, los, his):
    me_docs = lax.axis_index("docs")
    me_feat = lax.axis_index("feat")
    sub = docs // 128
    base = me_docs * (tiles * TILE)
    iota_lo = lax.broadcasted_iota(jnp.int32, (TILE, 128), 0).astype(jnp.bfloat16)
    iota_hi = lax.broadcasted_iota(jnp.int32, (tiles, 128), 0).astype(jnp.bfloat16)
    one_lo = jnp.ones((TILE, 128), jnp.bfloat16)
    zero_lo = jnp.zeros((TILE, 128), jnp.bfloat16)
    zero_hi = jnp.zeros((tiles, 128), jnp.bfloat16)
    lane = lax.broadcasted_iota(jnp.int32, (1, 128), 1)
    sums[...] = jnp.zeros_like(sums)

    def step(i, _):
        block = targets_ref[pl.ds(pl.multiple_of(i * step_rows, 8), step_rows), :] - base
        for r in range(step_rows):
            span = slice(r * 128, (r + 1) * 128)
            dev = ((i * step_rows + r) // rows_dev).astype(jnp.float32)
            dev_row = jnp.full((tiles, 128), dev, jnp.float32).astype(jnp.bfloat16)
            row = block[r:r + 1, :]
            hi = (row >> 7).astype(jnp.float32).astype(jnp.bfloat16)
            lo = (row & 127).astype(jnp.float32).astype(jnp.bfloat16)
            place = ((r % sub) * 128 + lane) ^ (me_feat * shard)
            place = place.astype(jnp.float32).astype(jnp.bfloat16)
            los[:, span] = jnp.where(iota_lo == lo, one_lo, zero_lo)
            here = iota_hi == hi
            his[:tiles, span] = jnp.where(here, jnp.broadcast_to(place, (tiles, 128)), zero_hi)
            his[tiles:, span] = jnp.where(here, dev_row, zero_hi)
        sums[...] += lax.dot_general(
            los[...], his[...], (((1,), (1,)), ((), ())), preferred_element_type=jnp.float32
        )
        return 0

    lax.fori_loop(0, targets_ref.shape[0] // step_rows, step, 0)
    out_ref[...] = sums[:, :tiles] + sums[:, tiles:] * docs


def _sources(targets, docs, tiles, rows_dev, shard):
    step_rows = _fits(targets.shape[0], 32)
    return pl.pallas_call(
        functools.partial(_source_kernel, docs, tiles, rows_dev, shard, step_rows),
        out_shape=jax.ShapeDtypeStruct((TILE, tiles), jnp.float32),
        in_specs=[pl.BlockSpec(memory_space=pltpu.VMEM)],
        out_specs=pl.BlockSpec(memory_space=pltpu.VMEM),
        scratch_shapes=[
            pltpu.VMEM((TILE, 2 * tiles), jnp.float32),
            pltpu.VMEM((TILE, step_rows * 128), jnp.bfloat16),
            pltpu.VMEM((2 * tiles, step_rows * 128), jnp.bfloat16),
        ],
        compiler_params=pltpu.CompilerParams(vmem_limit_bytes=VMEM_SMALL),
        cost_estimate=pl.CostEstimate(
            flops=2 * targets.size * TILE * TILE, bytes_accessed=4 * targets.size, transcendentals=0
        ),
    )(targets)


def _choose(pick, source_ref, tiles, blocks, rows, period, offset):
    lane = lax.broadcasted_iota(jnp.int32, (TILE, rows), 1).astype(jnp.bfloat16)
    one = jnp.ones((TILE, rows), jnp.bfloat16)
    zero = jnp.zeros((TILE, rows), jnp.bfloat16)
    for j, t in enumerate(tiles):
        s = jnp.broadcast_to(source_ref[:, t:t + 1], (TILE, rows))
        for b in range(blocks):
            here = (s - (b * period + offset)).astype(jnp.bfloat16)
            pick[j * TILE:(j + 1) * TILE, b * rows:(b + 1) * rows] = jnp.where(lane == here, one, zero)


def _collect(units, unit_refs):
    rows = unit_refs[0].shape[0]
    for b, ref in enumerate(unit_refs):
        units[b * rows:(b + 1) * rows, :] = ref[...]


def _place_kernel(blocks, group, period, offset, source_ref, *rest):
    unit_refs = rest[:blocks]
    table, units, pick = rest[blocks:]
    rows = unit_refs[0].shape[0]
    _collect(units, unit_refs)
    groups = table.shape[0] // (group * TILE)
    for g in range(-1, groups):
        if g + 1 < groups:
            span = range((g + 1) * group, (g + 2) * group)
            _choose(pick.at[(g + 1) % 2], source_ref, span, blocks, rows, period, offset)
        if g >= 0:
            table[g * group * TILE:(g + 1) * group * TILE, :] = jnp.dot(
                pick[g % 2], units[...], preferred_element_type=jnp.float32
            ).astype(jnp.bfloat16)


def _place(source, units, period, offset):
    tiles = source.shape[1]
    group = _fits(tiles, 4)
    rows, width = units[0].shape
    return pl.pallas_call(
        functools.partial(_place_kernel, len(units), group, period, offset),
        out_shape=jax.ShapeDtypeStruct((tiles * TILE, width), jnp.bfloat16),
        in_specs=[pl.BlockSpec(memory_space=pltpu.VMEM)] * (1 + len(units)),
        out_specs=pl.BlockSpec(memory_space=pltpu.VMEM),
        scratch_shapes=[
            pltpu.VMEM((len(units) * rows, width), jnp.bfloat16),
            pltpu.VMEM((2, group * TILE, len(units) * rows), jnp.bfloat16),
        ],
        compiler_params=pltpu.CompilerParams(vmem_limit_bytes=VMEM_TILES),
        cost_estimate=pl.CostEstimate(
            flops=2 * tiles * TILE * width * len(units) * rows,
            bytes_accessed=2 * tiles * TILE * width, transcendentals=0,
        ),
    )(source, *units)


def _tiles_kernel(blocks, group, period, offset, has_placed, counts_ref, source_ref, *rest):
    unit_refs = rest[:blocks]
    placed_ref = rest[blocks] if has_placed else None
    cosine_hbm, affinity_ref, cosine, units, pick, table, sems = rest[blocks + has_placed:]
    tiles = cosine.shape[0]
    rows = unit_refs[0].shape[0]
    row_of = lax.broadcasted_iota(jnp.int32, (TILE, TILE), 0)
    col_of = lax.broadcasted_iota(jnp.int32, (TILE, TILE), 1)
    _collect(units, unit_refs)

    def copy_out(g):
        span = pl.ds(g * group, group)
        return pltpu.make_async_copy(cosine.at[span], cosine_hbm.at[span], sems.at[g])

    def place(g):
        span = slice(g * group * TILE, (g + 1) * group * TILE)
        new = jnp.dot(pick[g % 2], units[...], preferred_element_type=jnp.float32).astype(jnp.bfloat16)
        table[span, :] = new + placed_ref[span, :] if has_placed else new

    def multiply(g):
        for t in range(g * group, (g + 1) * group):
            slots = table[t * TILE:(t + 1) * TILE, :]
            filled = counts_ref[t, 0]
            products = lax.dot_general(
                slots, slots, (((1,), (1,)), ((), ())), preferred_element_type=jnp.float32
            )
            products = jnp.where(jnp.maximum(row_of, col_of) < filled, products, 0.0)
            cosine[t] = products
            others = jnp.sum(jnp.where(row_of == col_of, 0.0, products), axis=0, keepdims=True)
            divisor = jnp.full((1, TILE), jnp.maximum(filled - 1, 1).astype(jnp.float32))
            affinity_ref[t:t + 1, :] = others / divisor
        copy_out(g).start()

    groups = tiles // group
    for g in range(-1, groups + 1):
        if g + 1 < groups:
            span = range((g + 1) * group, (g + 2) * group)
            _choose(pick.at[(g + 1) % 2], source_ref, span, blocks, rows, period, offset)
        if 0 <= g < groups:
            place(g)
        if g >= 1:
            multiply(g - 1)
    for g in range(groups):
        copy_out(g).wait()


def _tiles(counts, source, units, placed, period, offset):
    tiles = counts.shape[0]
    group = _fits(tiles, 4)
    rows, width = units[0].shape
    extra = [] if placed is None else [placed]
    return pl.pallas_call(
        functools.partial(_tiles_kernel, len(units), group, period, offset, len(extra)),
        out_shape=[
            jax.ShapeDtypeStruct((tiles, TILE, TILE), jnp.float32),
            jax.ShapeDtypeStruct((tiles, TILE), jnp.float32),
        ],
        in_specs=[pl.BlockSpec(memory_space=pltpu.SMEM)]
        + [pl.BlockSpec(memory_space=pltpu.VMEM)] * (1 + len(units) + len(extra)),
        out_specs=[pl.BlockSpec(memory_space=pl.ANY), pl.BlockSpec(memory_space=pltpu.VMEM)],
        scratch_shapes=[
            pltpu.VMEM((tiles, TILE, TILE), jnp.float32),
            pltpu.VMEM((len(units) * rows, width), jnp.bfloat16),
            pltpu.VMEM((2, group * TILE, len(units) * rows), jnp.bfloat16),
            pltpu.VMEM((tiles * TILE, width), jnp.bfloat16),
            pltpu.SemaphoreType.DMA((tiles // group,)),
        ],
        compiler_params=pltpu.CompilerParams(vmem_limit_bytes=VMEM_TILES),
        cost_estimate=pl.CostEstimate(
            flops=2 * tiles * TILE * width * (len(units) * rows + TILE),
            bytes_accessed=4 * tiles * TILE * TILE, transcendentals=0,
        ),
    )(counts, source, *units, *extra)


def solution(mesh):
    n_docs, n_feat = mesh.shape["docs"], mesh.shape["feat"]

    def send(x, axis, size, k):
        return lax.ppermute(x, axis, [(i, i ^ k) for i in range(size)])

    def everywhere(x, axis, size, step):
        return [x] + [send(x, axis, size, k) for k in range(step, size, step)]

    def per_device(ids, w, projection, lists, counts):
        docs = ids.shape[0]
        tiles = counts.shape[0]
        shard = docs // n_feat

        def targets_of(block):
            return (block[:, :, 0] * (tiles * TILE) + block[:, :, 1]).T.reshape(-1, 128)

        own = _signature_parts(ids, w, projection, n_feat, 0, docs)
        received = [send(own[k], "feat", n_feat, k) for k in range(1, n_feat)]
        lists, first = lax.optimization_barrier((lists, own[0] + received[0]))
        near_lists = jnp.stack(everywhere(targets_of(lists), "docs", n_docs, 2))
        rows_dev = near_lists.shape[1]
        unit = jnp.concatenate(everywhere(_unit([first] + received[1:]), "feat", n_feat, 1))
        unit, near_lists = lax.optimization_barrier((unit, near_lists))
        far = [send(unit, "docs", n_docs, k) for k in range(2, n_docs, 2)]
        targets = jnp.stack([near_lists, send(near_lists, "docs", n_docs, 1)], axis=1).reshape(-1, 128)
        source = _sources(targets, docs, tiles, rows_dev, shard)
        placed = _place(source, [unit, send(unit, "docs", n_docs, 1)], docs, 0)
        far, placed = lax.optimization_barrier((far, placed))
        units = [u for x in far for u in (x, send(x, "docs", n_docs, 1))]
        cosine, affinity = _tiles(counts, source, units, placed, docs, 2 * docs)
        return cosine[:, None], affinity[:, None]

    placed = (
        P("docs", "feat"),
        P("docs", "feat"),
        P("feat", None),
        P("docs", "feat", None),
        P("docs", "feat"),
    )
    return jax.shard_map(
        per_device,
        mesh=mesh,
        in_specs=placed,
        out_specs=(P("docs", "feat", None, None), P("docs", "feat", None)),
        check_vma=False,
    )
```

```python
import functools

import jax
import jax.numpy as jnp
from jax import lax
from jax.experimental import pallas as pl
from jax.experimental.pallas import tpu as pltpu
from jax.sharding import PartitionSpec as P

TILE = 128
LO = 128
EPSILON = 1e-06
VMEM_SMALL = 8 << 20
VMEM_SIGNATURE = 60 << 20
VMEM_TILES = 24 << 20


def _fits(count, most):
    while count % most:
        most -= 1
    return most


def _signature_kernel(
    first, docs, entries, hi_n, stride, unroll, k_step, parts,
    ids_ref, w_ref, proj_ref, *rest,
):
    out_refs = rest[:parts]
    proj, counts, lhs, weights, total, sems = rest[parts:]
    chunks, chunk_rows, _ = proj.shape

    def chunk_copy(c):
        return pltpu.make_async_copy(
            proj_ref.at[pl.ds(c * chunk_rows, chunk_rows), :], proj.at[c], sems.at[c]
        )

    for c in range(chunks):
        chunk_copy(c).start()
    weights[...] = w_ref[first:first + docs, :].astype(jnp.float32)

    def pair(p):
        iota_hi = lax.broadcasted_iota(jnp.int32, (hi_n, entries), 0).astype(jnp.bfloat16)
        iota_lo = lax.broadcasted_iota(jnp.int32, (LO, entries), 0).astype(jnp.bfloat16)
        one_hi = jnp.ones((hi_n, entries), jnp.bfloat16)
        zero_hi = jnp.zeros((hi_n, entries), jnp.bfloat16)
        zero_lo = jnp.zeros((LO, entries), jnp.bfloat16)
        his, los = [], []
        for e in range(2):
            ids = ids_ref[pl.ds(first + 2 * p + e, 1), :]
            w = weights[pl.ds(2 * p + e, 1), :].astype(jnp.bfloat16)
            hi = (ids // LO).astype(jnp.float32).astype(jnp.bfloat16)
            lo = (ids % LO).astype(jnp.float32).astype(jnp.bfloat16)
            his.append(jnp.where(iota_hi == hi, one_hi, zero_hi))
            lo_w = jnp.where(iota_lo == lo, jnp.broadcast_to(w, (LO, entries)), zero_lo)
            los.append(jnp.concatenate([lo_w, zero_lo] if e == 0 else [zero_lo, lo_w], axis=1))
        r = lax.dot_general(
            jnp.concatenate(his, axis=1), jnp.concatenate(los, axis=0),
            (((1,), (1,)), ((), ())), preferred_element_type=jnp.float32,
        )
        for e in range(2):
            for t in range(hi_n // 8):
                counts[pl.ds(t * 8 * stride + 2 * p + e, 8, stride=stride), :] = r[
                    t * 8:(t + 1) * 8, e * LO:(e + 1) * LO
                ]

    def pairs(i, _):
        for u in range(unroll):
            pair(i * unroll + u)
        return 0

    lax.fori_loop(0, docs // 2 // unroll, pairs, 0)

    per_chunk = chunk_rows // LO
    for c in range(chunks):
        chunk_copy(c).wait()

        def multiply(k, _, c=c):
            for q in range(k_step):
                row = pl.multiple_of((c * per_chunk + k_step * k + q) * stride, 8)
                a = counts[pl.ds(row, docs), :]
                top = a.astype(jnp.bfloat16)
                lhs[:docs, q * LO:(q + 1) * LO] = top
                lhs[docs:, q * LO:(q + 1) * LO] = (a - top.astype(jnp.float32)).astype(jnp.bfloat16)
            feature = pl.multiple_of(k * k_step * LO, k_step * LO)
            r = jnp.dot(
                lhs[...], proj[c, pl.ds(feature, k_step * LO), :],
                preferred_element_type=jnp.float32,
            )
            r = r[:docs] + r[docs:]
            if c == 0:
                total[...] = jnp.where(k == 0, r, total[...] + r)
            else:
                total[...] += r
            return 0

        lax.fori_loop(0, per_chunk // k_step, multiply, 0)

    part_rows = docs // parts
    me = lax.axis_index("feat")
    for k in range(parts):
        row = pl.multiple_of((me ^ k) * part_rows, part_rows)
        out_refs[k][...] = total[pl.ds(row, part_rows), :]


def _signature_parts(ids, w, projection, parts, first, docs):
    entries = ids.shape[1]
    feats, width = projection.shape
    hi_n = feats // LO
    chunks = 2
    stride = docs + 8
    k_step = _fits(hi_n // chunks, 64)
    unroll = _fits(docs // 2, 64)
    return pl.pallas_call(
        functools.partial(
            _signature_kernel, first, docs, entries, hi_n, stride, unroll, k_step, parts
        ),
        out_shape=[jax.ShapeDtypeStruct((docs // parts, width), jnp.float32)] * parts,
        in_specs=[
            pl.BlockSpec(memory_space=pltpu.VMEM),
            pl.BlockSpec(memory_space=pltpu.VMEM),
            pl.BlockSpec(memory_space=pl.ANY),
        ],
        out_specs=[pl.BlockSpec(memory_space=pltpu.VMEM)] * parts,
        scratch_shapes=[
            pltpu.VMEM((chunks, feats // chunks, width), jnp.bfloat16),
            pltpu.VMEM((hi_n * stride, LO), jnp.float32),
            pltpu.VMEM((2 * docs, k_step * LO), jnp.bfloat16),
            pltpu.VMEM((docs, entries), jnp.float32),
            pltpu.VMEM((docs, width), jnp.float32),
            pltpu.SemaphoreType.DMA((chunks,)),
        ],
        compiler_params=pltpu.CompilerParams(vmem_limit_bytes=VMEM_SIGNATURE),
        cost_estimate=pl.CostEstimate(
            flops=6 * docs * feats * width, bytes_accessed=2 * feats * width, transcendentals=0
        ),
    )(ids, w, projection)


def _unit_kernel(*refs):
    total = refs[0][...]
    for ref in refs[1:-1]:
        total = total + ref[...]
    scale = lax.rsqrt(jnp.sum(total * total, axis=1, keepdims=True) + EPSILON)
    refs[-1][...] = (total * scale).astype(jnp.bfloat16)


def _unit(parts):
    return pl.pallas_call(
        _unit_kernel,
        out_shape=jax.ShapeDtypeStruct(parts[0].shape, jnp.bfloat16),
        in_specs=[pl.BlockSpec(memory_space=pltpu.VMEM)] * len(parts),
        out_specs=pl.BlockSpec(memory_space=pltpu.VMEM),
        compiler_params=pltpu.CompilerParams(vmem_limit_bytes=VMEM_SMALL),
    )(*parts)


def _source_kernel(docs, tiles, rows_dev, shard, step_rows, targets_ref, out_ref, sums, los, his):
    me_docs = lax.axis_index("docs")
    me_feat = lax.axis_index("feat")
    sub = docs // 128
    base = me_docs * (tiles * TILE)
    iota_lo = lax.broadcasted_iota(jnp.int32, (TILE, 128), 0).astype(jnp.bfloat16)
    iota_hi = lax.broadcasted_iota(jnp.int32, (tiles, 128), 0).astype(jnp.bfloat16)
    one_lo = jnp.ones((TILE, 128), jnp.bfloat16)
    zero_lo = jnp.zeros((TILE, 128), jnp.bfloat16)
    zero_hi = jnp.zeros((tiles, 128), jnp.bfloat16)
    lane = lax.broadcasted_iota(jnp.int32, (1, 128), 1)
    sums[...] = jnp.zeros_like(sums)

    def step(i, _):
        block = targets_ref[pl.ds(pl.multiple_of(i * step_rows, 8), step_rows), :] - base
        for r in range(step_rows):
            span = slice(r * 128, (r + 1) * 128)
            dev = ((i * step_rows + r) // rows_dev).astype(jnp.float32)
            dev_row = jnp.full((tiles, 128), dev, jnp.float32).astype(jnp.bfloat16)
            row = block[r:r + 1, :]
            hi = (row >> 7).astype(jnp.float32).astype(jnp.bfloat16)
            lo = (row & 127).astype(jnp.float32).astype(jnp.bfloat16)
            place = ((r % sub) * 128 + lane) ^ (me_feat * shard)
            place = place.astype(jnp.float32).astype(jnp.bfloat16)
            los[:, span] = jnp.where(iota_lo == lo, one_lo, zero_lo)
            here = iota_hi == hi
            his[:tiles, span] = jnp.where(here, jnp.broadcast_to(place, (tiles, 128)), zero_hi)
            his[tiles:, span] = jnp.where(here, dev_row, zero_hi)
        sums[...] += lax.dot_general(
            los[...], his[...], (((1,), (1,)), ((), ())), preferred_element_type=jnp.float32
        )
        return 0

    lax.fori_loop(0, targets_ref.shape[0] // step_rows, step, 0)
    out_ref[...] = sums[:, :tiles] + sums[:, tiles:] * docs


def _sources(targets, docs, tiles, rows_dev, shard):
    step_rows = _fits(targets.shape[0], 32)
    return pl.pallas_call(
        functools.partial(_source_kernel, docs, tiles, rows_dev, shard, step_rows),
        out_shape=jax.ShapeDtypeStruct((TILE, tiles), jnp.float32),
        in_specs=[pl.BlockSpec(memory_space=pltpu.VMEM)],
        out_specs=pl.BlockSpec(memory_space=pltpu.VMEM),
        scratch_shapes=[
            pltpu.VMEM((TILE, 2 * tiles), jnp.float32),
            pltpu.VMEM((TILE, step_rows * 128), jnp.bfloat16),
            pltpu.VMEM((2 * tiles, step_rows * 128), jnp.bfloat16),
        ],
        compiler_params=pltpu.CompilerParams(vmem_limit_bytes=VMEM_SMALL),
        cost_estimate=pl.CostEstimate(
            flops=2 * targets.size * TILE * TILE, bytes_accessed=4 * targets.size, transcendentals=0
        ),
    )(targets)


def _choose(pick, source_ref, tiles, starts, rows):
    lane = lax.broadcasted_iota(jnp.int32, (TILE, rows), 1).astype(jnp.bfloat16)
    one = jnp.ones((TILE, rows), jnp.bfloat16)
    zero = jnp.zeros((TILE, rows), jnp.bfloat16)
    for j, t in enumerate(tiles):
        s = jnp.broadcast_to(source_ref[:, t:t + 1], (TILE, rows))
        for b, start in enumerate(starts):
            here = (s - start).astype(jnp.bfloat16)
            pick[j * TILE:(j + 1) * TILE, b * rows:(b + 1) * rows] = jnp.where(lane == here, one, zero)


def _collect(units, unit_refs):
    rows = unit_refs[0].shape[0]
    for b, ref in enumerate(unit_refs):
        units[b * rows:(b + 1) * rows, :] = ref[...]


def _place_kernel(starts, group, has_placed, source_ref, *rest):
    blocks = len(starts)
    unit_refs = rest[:blocks]
    placed_ref = rest[blocks] if has_placed else None
    table, units, pick = rest[blocks + has_placed:]
    rows = unit_refs[0].shape[0]
    _collect(units, unit_refs)
    groups = table.shape[0] // (group * TILE)
    for g in range(-1, groups):
        if g + 1 < groups:
            span = range((g + 1) * group, (g + 2) * group)
            _choose(pick.at[(g + 1) % 2], source_ref, span, starts, rows)
        if g >= 0:
            span = slice(g * group * TILE, (g + 1) * group * TILE)
            new = jnp.dot(pick[g % 2], units[...], preferred_element_type=jnp.float32).astype(jnp.bfloat16)
            table[span, :] = new + placed_ref[span, :] if has_placed else new


def _place(source, units, starts, placed):
    tiles = source.shape[1]
    group = _fits(tiles, 4)
    rows, width = units[0].shape
    extra = [] if placed is None else [placed]
    return pl.pallas_call(
        functools.partial(_place_kernel, starts, group, len(extra)),
        out_shape=jax.ShapeDtypeStruct((tiles * TILE, width), jnp.bfloat16),
        in_specs=[pl.BlockSpec(memory_space=pltpu.VMEM)] * (1 + len(units) + len(extra)),
        out_specs=pl.BlockSpec(memory_space=pltpu.VMEM),
        scratch_shapes=[
            pltpu.VMEM((len(units) * rows, width), jnp.bfloat16),
            pltpu.VMEM((2, group * TILE, len(units) * rows), jnp.bfloat16),
        ],
        compiler_params=pltpu.CompilerParams(vmem_limit_bytes=VMEM_TILES),
        cost_estimate=pl.CostEstimate(
            flops=2 * tiles * TILE * width * len(units) * rows,
            bytes_accessed=2 * tiles * TILE * width, transcendentals=0,
        ),
    )(source, *units, *extra)


def _tiles_kernel(starts, group, has_placed, counts_ref, source_ref, *rest):
    blocks = len(starts)
    unit_refs = rest[:blocks]
    placed_ref = rest[blocks] if has_placed else None
    cosine_hbm, affinity_ref, cosine, units, pick, table, sems = rest[blocks + has_placed:]
    tiles = cosine.shape[0]
    rows = unit_refs[0].shape[0]
    row_of = lax.broadcasted_iota(jnp.int32, (TILE, TILE), 0)
    col_of = lax.broadcasted_iota(jnp.int32, (TILE, TILE), 1)
    _collect(units, unit_refs)

    def copy_out(g):
        span = pl.ds(g * group, group)
        return pltpu.make_async_copy(cosine.at[span], cosine_hbm.at[span], sems.at[g])

    def place(g):
        span = slice(g * group * TILE, (g + 1) * group * TILE)
        new = jnp.dot(pick[g % 2], units[...], preferred_element_type=jnp.float32).astype(jnp.bfloat16)
        table[span, :] = new + placed_ref[span, :] if has_placed else new

    def multiply(g):
        for t in range(g * group, (g + 1) * group):
            slots = table[t * TILE:(t + 1) * TILE, :]
            filled = counts_ref[t, 0]
            products = lax.dot_general(
                slots, slots, (((1,), (1,)), ((), ())), preferred_element_type=jnp.float32
            )
            products = jnp.where(jnp.maximum(row_of, col_of) < filled, products, 0.0)
            cosine[t] = products
            others = jnp.sum(jnp.where(row_of == col_of, 0.0, products), axis=0, keepdims=True)
            divisor = jnp.full((1, TILE), jnp.maximum(filled - 1, 1).astype(jnp.float32))
            affinity_ref[t:t + 1, :] = others / divisor
        copy_out(g).start()

    groups = tiles // group
    for g in range(-1, groups + 1):
        if g + 1 < groups:
            span = range((g + 1) * group, (g + 2) * group)
            _choose(pick.at[(g + 1) % 2], source_ref, span, starts, rows)
        if 0 <= g < groups:
            place(g)
        if g >= 1:
            multiply(g - 1)
    for g in range(groups):
        copy_out(g).wait()


def _tiles(counts, source, units, starts, placed):
    tiles = counts.shape[0]
    group = _fits(tiles, 4)
    rows, width = units[0].shape
    extra = [] if placed is None else [placed]
    return pl.pallas_call(
        functools.partial(_tiles_kernel, starts, group, len(extra)),
        out_shape=[
            jax.ShapeDtypeStruct((tiles, TILE, TILE), jnp.float32),
            jax.ShapeDtypeStruct((tiles, TILE), jnp.float32),
        ],
        in_specs=[pl.BlockSpec(memory_space=pltpu.SMEM)]
        + [pl.BlockSpec(memory_space=pltpu.VMEM)] * (1 + len(units) + len(extra)),
        out_specs=[pl.BlockSpec(memory_space=pl.ANY), pl.BlockSpec(memory_space=pltpu.VMEM)],
        scratch_shapes=[
            pltpu.VMEM((tiles, TILE, TILE), jnp.float32),
            pltpu.VMEM((len(units) * rows, width), jnp.bfloat16),
            pltpu.VMEM((2, group * TILE, len(units) * rows), jnp.bfloat16),
            pltpu.VMEM((tiles * TILE, width), jnp.bfloat16),
            pltpu.SemaphoreType.DMA((tiles // group,)),
        ],
        compiler_params=pltpu.CompilerParams(vmem_limit_bytes=VMEM_TILES),
        cost_estimate=pl.CostEstimate(
            flops=2 * tiles * TILE * width * (len(units) * rows + TILE),
            bytes_accessed=4 * tiles * TILE * TILE, transcendentals=0,
        ),
    )(counts, source, *units, *extra)


def solution(mesh):
    n_docs, n_feat = mesh.shape["docs"], mesh.shape["feat"]

    def send(x, axis, size, k):
        return lax.ppermute(x, axis, [(i, i ^ k) for i in range(size)])

    def everywhere(x, axis, size, step):
        return [x] + [send(x, axis, size, k) for k in range(step, size, step)]

    def per_device(ids, w, projection, lists, counts):
        docs = ids.shape[0]
        tiles = counts.shape[0]
        shard = docs // n_feat

        def targets_of(block):
            return (block[:, :, 0] * (tiles * TILE) + block[:, :, 1]).T.reshape(-1, 128)

        own = _signature_parts(ids, w, projection, n_feat, 0, docs)
        received = [send(own[k], "feat", n_feat, k) for k in range(1, n_feat)]
        lists, first = lax.optimization_barrier((lists, own[0] + received[0]))
        near_lists = jnp.stack(everywhere(targets_of(lists), "docs", n_docs, 2))
        rows_dev = near_lists.shape[1]
        shards = everywhere(_unit([first] + received[1:]), "feat", n_feat, 1)
        unit = jnp.zeros((docs, shards[0].shape[1]), jnp.bfloat16)
        for k in reversed(range(n_feat)):
            unit = lax.dynamic_update_slice(unit, shards[k], (k * shard, 0))
        unit, near_lists = lax.optimization_barrier((unit, near_lists))
        far = [send(unit, "docs", n_docs, k) for k in range(2, n_docs, 2)]
        targets = jnp.stack([near_lists, send(near_lists, "docs", n_docs, 1)], axis=1).reshape(-1, 128)
        source = _sources(targets, docs, tiles, rows_dev, shard)

        def swap(x):
            return send(x, "docs", n_docs, 1)

        at = [docs * k for k in range(n_docs)]
        placed = _place(source, [unit, swap(unit)], at[:2], None)
        near, placed = lax.optimization_barrier((far[0], placed))
        first = swap(near)
        placed = _place(source, [near], at[2:3], placed)
        rest, placed = lax.optimization_barrier((far[1:], placed))
        swapped = [swap(x) for x in rest]
        placed = _place(source, rest + [first], at[4::2] + at[3:4], placed)
        cosine, affinity = _tiles(counts, source, swapped, at[5::2], placed)
        return cosine[:, None], affinity[:, None]

    placed = (
        P("docs", "feat"),
        P("docs", "feat"),
        P("feat", None),
        P("docs", "feat", None),
        P("docs", "feat"),
    )
    return jax.shard_map(
        per_device,
        mesh=mesh,
        in_specs=placed,
        out_specs=(P("docs", "feat", None, None), P("docs", "feat", None)),
        check_vma=False,
    )
```

```python
import functools

import jax
import jax.numpy as jnp
from jax import lax
from jax.experimental import pallas as pl
from jax.experimental.pallas import tpu as pltpu
from jax.sharding import PartitionSpec as P

TILE = 128
LO = 128
EPSILON = 1e-06
VMEM_SMALL = 8 << 20
VMEM_SIGNATURE = 60 << 20
VMEM_TILES = 24 << 20


def _fits(count, most):
    while count % most:
        most -= 1
    return most


def _signature_kernel(
    first, docs, entries, hi_n, stride, unroll, k_step, parts,
    ids_ref, w_ref, proj_ref, *rest,
):
    out_refs = rest[:parts]
    proj, counts, lhs, weights, total, sems = rest[parts:]
    chunks, chunk_rows, _ = proj.shape

    def chunk_copy(c):
        return pltpu.make_async_copy(
            proj_ref.at[pl.ds(c * chunk_rows, chunk_rows), :], proj.at[c], sems.at[c]
        )

    for c in range(chunks):
        chunk_copy(c).start()
    weights[...] = w_ref[first:first + docs, :].astype(jnp.float32)

    def pair(p):
        iota_hi = lax.broadcasted_iota(jnp.int32, (hi_n, entries), 0).astype(jnp.bfloat16)
        iota_lo = lax.broadcasted_iota(jnp.int32, (LO, entries), 0).astype(jnp.bfloat16)
        one_hi = jnp.ones((hi_n, entries), jnp.bfloat16)
        zero_hi = jnp.zeros((hi_n, entries), jnp.bfloat16)
        zero_lo = jnp.zeros((LO, entries), jnp.bfloat16)
        his, los = [], []
        for e in range(2):
            ids = ids_ref[pl.ds(first + 2 * p + e, 1), :]
            w = weights[pl.ds(2 * p + e, 1), :].astype(jnp.bfloat16)
            hi = (ids // LO).astype(jnp.float32).astype(jnp.bfloat16)
            lo = (ids % LO).astype(jnp.float32).astype(jnp.bfloat16)
            his.append(jnp.where(iota_hi == hi, one_hi, zero_hi))
            lo_w = jnp.where(iota_lo == lo, jnp.broadcast_to(w, (LO, entries)), zero_lo)
            los.append(jnp.concatenate([lo_w, zero_lo] if e == 0 else [zero_lo, lo_w], axis=1))
        r = lax.dot_general(
            jnp.concatenate(his, axis=1), jnp.concatenate(los, axis=0),
            (((1,), (1,)), ((), ())), preferred_element_type=jnp.float32,
        )
        for e in range(2):
            for t in range(hi_n // 8):
                counts[pl.ds(t * 8 * stride + 2 * p + e, 8, stride=stride), :] = r[
                    t * 8:(t + 1) * 8, e * LO:(e + 1) * LO
                ]

    def pairs(i, _):
        for u in range(unroll):
            pair(i * unroll + u)
        return 0

    lax.fori_loop(0, docs // 2 // unroll, pairs, 0)

    per_chunk = chunk_rows // LO
    for c in range(chunks):
        chunk_copy(c).wait()

        def multiply(k, _, c=c):
            for q in range(k_step):
                row = pl.multiple_of((c * per_chunk + k_step * k + q) * stride, 8)
                a = counts[pl.ds(row, docs), :]
                top = a.astype(jnp.bfloat16)
                lhs[:docs, q * LO:(q + 1) * LO] = top
                lhs[docs:, q * LO:(q + 1) * LO] = (a - top.astype(jnp.float32)).astype(jnp.bfloat16)
            feature = pl.multiple_of(k * k_step * LO, k_step * LO)
            r = jnp.dot(
                lhs[...], proj[c, pl.ds(feature, k_step * LO), :],
                preferred_element_type=jnp.float32,
            )
            r = r[:docs] + r[docs:]
            if c == 0:
                total[...] = jnp.where(k == 0, r, total[...] + r)
            else:
                total[...] += r
            return 0

        lax.fori_loop(0, per_chunk // k_step, multiply, 0)

    part_rows = docs // parts
    me = lax.axis_index("feat")
    for k in range(parts):
        row = pl.multiple_of((me ^ k) * part_rows, part_rows)
        out_refs[k][...] = total[pl.ds(row, part_rows), :]


def _signature_parts(ids, w, projection, parts, first, docs):
    entries = ids.shape[1]
    feats, width = projection.shape
    hi_n = feats // LO
    chunks = 2
    stride = docs + 8
    k_step = _fits(hi_n // chunks, 64)
    unroll = _fits(docs // 2, 64)
    return pl.pallas_call(
        functools.partial(
            _signature_kernel, first, docs, entries, hi_n, stride, unroll, k_step, parts
        ),
        out_shape=[jax.ShapeDtypeStruct((docs // parts, width), jnp.float32)] * parts,
        in_specs=[
            pl.BlockSpec(memory_space=pltpu.VMEM),
            pl.BlockSpec(memory_space=pltpu.VMEM),
            pl.BlockSpec(memory_space=pl.ANY),
        ],
        out_specs=[pl.BlockSpec(memory_space=pltpu.VMEM)] * parts,
        scratch_shapes=[
            pltpu.VMEM((chunks, feats // chunks, width), jnp.bfloat16),
            pltpu.VMEM((hi_n * stride, LO), jnp.float32),
            pltpu.VMEM((2 * docs, k_step * LO), jnp.bfloat16),
            pltpu.VMEM((docs, entries), jnp.float32),
            pltpu.VMEM((docs, width), jnp.float32),
            pltpu.SemaphoreType.DMA((chunks,)),
        ],
        compiler_params=pltpu.CompilerParams(vmem_limit_bytes=VMEM_SIGNATURE),
        cost_estimate=pl.CostEstimate(
            flops=6 * docs * feats * width, bytes_accessed=2 * feats * width, transcendentals=0
        ),
    )(ids, w, projection)


def _unit_kernel(*refs):
    total = refs[0][...]
    for ref in refs[1:-1]:
        total = total + ref[...]
    scale = lax.rsqrt(jnp.sum(total * total, axis=1, keepdims=True) + EPSILON)
    refs[-1][...] = (total * scale).astype(jnp.bfloat16)


def _unit(parts):
    return pl.pallas_call(
        _unit_kernel,
        out_shape=jax.ShapeDtypeStruct(parts[0].shape, jnp.bfloat16),
        in_specs=[pl.BlockSpec(memory_space=pltpu.VMEM)] * len(parts),
        out_specs=pl.BlockSpec(memory_space=pltpu.VMEM),
        compiler_params=pltpu.CompilerParams(vmem_limit_bytes=VMEM_SMALL),
    )(*parts)


def _source_kernel(docs, tiles, rows_dev, shard, step_rows, targets_ref, out_ref, sums, los, his):
    me_docs = lax.axis_index("docs")
    me_feat = lax.axis_index("feat")
    sub = docs // 128
    base = me_docs * (tiles * TILE)
    iota_lo = lax.broadcasted_iota(jnp.int32, (TILE, 128), 0).astype(jnp.bfloat16)
    iota_hi = lax.broadcasted_iota(jnp.int32, (tiles, 128), 0).astype(jnp.bfloat16)
    one_lo = jnp.ones((TILE, 128), jnp.bfloat16)
    zero_lo = jnp.zeros((TILE, 128), jnp.bfloat16)
    zero_hi = jnp.zeros((tiles, 128), jnp.bfloat16)
    lane = lax.broadcasted_iota(jnp.int32, (1, 128), 1)
    sums[...] = jnp.zeros_like(sums)

    def step(i, _):
        block = targets_ref[pl.ds(pl.multiple_of(i * step_rows, 8), step_rows), :] - base
        for r in range(step_rows):
            span = slice(r * 128, (r + 1) * 128)
            dev = ((i * step_rows + r) // rows_dev).astype(jnp.float32)
            dev_row = jnp.full((tiles, 128), dev, jnp.float32).astype(jnp.bfloat16)
            row = block[r:r + 1, :]
            hi = (row >> 7).astype(jnp.float32).astype(jnp.bfloat16)
            lo = (row & 127).astype(jnp.float32).astype(jnp.bfloat16)
            place = ((r % sub) * 128 + lane) ^ (me_feat * shard)
            place = place.astype(jnp.float32).astype(jnp.bfloat16)
            los[:, span] = jnp.where(iota_lo == lo, one_lo, zero_lo)
            here = iota_hi == hi
            his[:tiles, span] = jnp.where(here, jnp.broadcast_to(place, (tiles, 128)), zero_hi)
            his[tiles:, span] = jnp.where(here, dev_row, zero_hi)
        sums[...] += lax.dot_general(
            los[...], his[...], (((1,), (1,)), ((), ())), preferred_element_type=jnp.float32
        )
        return 0

    lax.fori_loop(0, targets_ref.shape[0] // step_rows, step, 0)
    out_ref[...] = sums[:, :tiles] + sums[:, tiles:] * docs


def _sources(targets, docs, tiles, rows_dev, shard):
    step_rows = _fits(targets.shape[0], 32)
    return pl.pallas_call(
        functools.partial(_source_kernel, docs, tiles, rows_dev, shard, step_rows),
        out_shape=jax.ShapeDtypeStruct((TILE, tiles), jnp.float32),
        in_specs=[pl.BlockSpec(memory_space=pltpu.VMEM)],
        out_specs=pl.BlockSpec(memory_space=pltpu.VMEM),
        scratch_shapes=[
            pltpu.VMEM((TILE, 2 * tiles), jnp.float32),
            pltpu.VMEM((TILE, step_rows * 128), jnp.bfloat16),
            pltpu.VMEM((2 * tiles, step_rows * 128), jnp.bfloat16),
        ],
        compiler_params=pltpu.CompilerParams(vmem_limit_bytes=VMEM_SMALL),
        cost_estimate=pl.CostEstimate(
            flops=2 * targets.size * TILE * TILE, bytes_accessed=4 * targets.size, transcendentals=0
        ),
    )(targets)


def _choose(pick, source_ref, tiles, starts, rows):
    lane = lax.broadcasted_iota(jnp.int32, (TILE, rows), 1).astype(jnp.bfloat16)
    one = jnp.ones((TILE, rows), jnp.bfloat16)
    zero = jnp.zeros((TILE, rows), jnp.bfloat16)
    for j, t in enumerate(tiles):
        s = jnp.broadcast_to(source_ref[:, t:t + 1], (TILE, rows))
        for b, start in enumerate(starts):
            here = (s - start).astype(jnp.bfloat16)
            pick[j * TILE:(j + 1) * TILE, b * rows:(b + 1) * rows] = jnp.where(lane == here, one, zero)


def _collect(units, unit_refs):
    rows = unit_refs[0].shape[0]
    for b, ref in enumerate(unit_refs):
        units[b * rows:(b + 1) * rows, :] = ref[...]


def _place_kernel(starts, group, has_placed, source_ref, *rest):
    blocks = len(starts)
    unit_refs = rest[:blocks]
    placed_ref = rest[blocks] if has_placed else None
    table, units, pick = rest[blocks + has_placed:]
    rows = unit_refs[0].shape[0]
    _collect(units, unit_refs)
    groups = table.shape[0] // (group * TILE)
    for g in range(-1, groups):
        if g + 1 < groups:
            span = range((g + 1) * group, (g + 2) * group)
            _choose(pick.at[(g + 1) % 2], source_ref, span, starts, rows)
        if g >= 0:
            span = slice(g * group * TILE, (g + 1) * group * TILE)
            new = jnp.dot(pick[g % 2], units[...], preferred_element_type=jnp.float32).astype(jnp.bfloat16)
            table[span, :] = new + placed_ref[span, :] if has_placed else new


def _place(source, units, starts, placed):
    tiles = source.shape[1]
    group = _fits(tiles, 4)
    rows, width = units[0].shape
    extra = [] if placed is None else [placed]
    return pl.pallas_call(
        functools.partial(_place_kernel, starts, group, len(extra)),
        out_shape=jax.ShapeDtypeStruct((tiles * TILE, width), jnp.bfloat16),
        in_specs=[pl.BlockSpec(memory_space=pltpu.VMEM)] * (1 + len(units) + len(extra)),
        out_specs=pl.BlockSpec(memory_space=pltpu.VMEM),
        scratch_shapes=[
            pltpu.VMEM((len(units) * rows, width), jnp.bfloat16),
            pltpu.VMEM((2, group * TILE, len(units) * rows), jnp.bfloat16),
        ],
        compiler_params=pltpu.CompilerParams(vmem_limit_bytes=VMEM_TILES),
        cost_estimate=pl.CostEstimate(
            flops=2 * tiles * TILE * width * len(units) * rows,
            bytes_accessed=2 * tiles * TILE * width, transcendentals=0,
        ),
    )(source, *units, *extra)


def _tiles_kernel(starts, group, has_placed, counts_ref, source_ref, *rest):
    blocks = len(starts)
    unit_refs = rest[:blocks]
    placed_ref = rest[blocks] if has_placed else None
    cosine_hbm, affinity_ref, cosine, units, pick, table, sems = rest[blocks + has_placed:]
    tiles = cosine.shape[0]
    rows = unit_refs[0].shape[0]
    row_of = lax.broadcasted_iota(jnp.int32, (TILE, TILE), 0)
    col_of = lax.broadcasted_iota(jnp.int32, (TILE, TILE), 1)
    _collect(units, unit_refs)

    def copy_out(g):
        span = pl.ds(g * group, group)
        return pltpu.make_async_copy(cosine.at[span], cosine_hbm.at[span], sems.at[g])

    def place(g):
        span = slice(g * group * TILE, (g + 1) * group * TILE)
        new = jnp.dot(pick[g % 2], units[...], preferred_element_type=jnp.float32).astype(jnp.bfloat16)
        table[span, :] = new + placed_ref[span, :] if has_placed else new

    def multiply(g):
        for t in range(g * group, (g + 1) * group):
            slots = table[t * TILE:(t + 1) * TILE, :]
            filled = counts_ref[t, 0]
            products = lax.dot_general(
                slots, slots, (((1,), (1,)), ((), ())), preferred_element_type=jnp.float32
            )
            products = jnp.where(jnp.maximum(row_of, col_of) < filled, products, 0.0)
            cosine[t] = products
            others = jnp.sum(jnp.where(row_of == col_of, 0.0, products), axis=0, keepdims=True)
            divisor = jnp.full((1, TILE), jnp.maximum(filled - 1, 1).astype(jnp.float32))
            affinity_ref[t:t + 1, :] = others / divisor
        copy_out(g).start()

    groups = tiles // group
    for g in range(-1, groups + 1):
        if g + 1 < groups:
            span = range((g + 1) * group, (g + 2) * group)
            _choose(pick.at[(g + 1) % 2], source_ref, span, starts, rows)
        if 0 <= g < groups:
            place(g)
        if g >= 1:
            multiply(g - 1)
    for g in range(groups):
        copy_out(g).wait()


def _tiles(counts, source, units, starts, placed):
    tiles = counts.shape[0]
    group = _fits(tiles, 4)
    rows, width = units[0].shape
    extra = [] if placed is None else [placed]
    return pl.pallas_call(
        functools.partial(_tiles_kernel, starts, group, len(extra)),
        out_shape=[
            jax.ShapeDtypeStruct((tiles, TILE, TILE), jnp.float32),
            jax.ShapeDtypeStruct((tiles, TILE), jnp.float32),
        ],
        in_specs=[pl.BlockSpec(memory_space=pltpu.SMEM)]
        + [pl.BlockSpec(memory_space=pltpu.VMEM)] * (1 + len(units) + len(extra)),
        out_specs=[pl.BlockSpec(memory_space=pl.ANY), pl.BlockSpec(memory_space=pltpu.VMEM)],
        scratch_shapes=[
            pltpu.VMEM((tiles, TILE, TILE), jnp.float32),
            pltpu.VMEM((len(units) * rows, width), jnp.bfloat16),
            pltpu.VMEM((2, group * TILE, len(units) * rows), jnp.bfloat16),
            pltpu.VMEM((tiles * TILE, width), jnp.bfloat16),
            pltpu.SemaphoreType.DMA((tiles // group,)),
        ],
        compiler_params=pltpu.CompilerParams(vmem_limit_bytes=VMEM_TILES),
        cost_estimate=pl.CostEstimate(
            flops=2 * tiles * TILE * width * (len(units) * rows + TILE),
            bytes_accessed=4 * tiles * TILE * TILE, transcendentals=0,
        ),
    )(counts, source, *units, *extra)


def solution(mesh):
    n_docs, n_feat = mesh.shape["docs"], mesh.shape["feat"]

    def send(x, axis, size, k):
        return lax.ppermute(x, axis, [(i, i ^ k) for i in range(size)])

    def everywhere(x, axis, size, step):
        return [x] + [send(x, axis, size, k) for k in range(step, size, step)]

    def per_device(ids, w, projection, lists, counts):
        docs = ids.shape[0]
        tiles = counts.shape[0]
        shard = docs // n_feat

        def targets_of(block):
            return (block[:, :, 0] * (tiles * TILE) + block[:, :, 1]).T.reshape(-1, 128)

        own = _signature_parts(ids, w, projection, n_feat, 0, docs)
        received = [send(own[k], "feat", n_feat, k) for k in range(1, n_feat)]
        lists, first = lax.optimization_barrier((lists, own[0] + received[0]))
        near_lists = jnp.stack(everywhere(targets_of(lists), "docs", n_docs, 2))
        rows_dev = near_lists.shape[1]
        shards = everywhere(_unit([first] + received[1:]), "feat", n_feat, 1)
        unit = jnp.zeros((docs, shards[0].shape[1]), jnp.bfloat16)
        for k in reversed(range(n_feat)):
            unit = lax.dynamic_update_slice(unit, shards[k], (k * shard, 0))
        unit, near_lists = lax.optimization_barrier((unit, near_lists))
        far = [send(unit, "docs", n_docs, k) for k in range(2, n_docs, 2)]
        targets = jnp.stack([near_lists, send(near_lists, "docs", n_docs, 1)], axis=1).reshape(-1, 128)
        source = _sources(targets, docs, tiles, rows_dev, shard)

        def swap(x):
            return send(x, "docs", n_docs, 1)

        at = [docs * k for k in range(n_docs)]
        placed = _place(source, [unit, swap(unit)], at[:2], None)
        near, placed = lax.optimization_barrier((far[-1], placed))
        first = swap(near)
        placed = _place(source, [near], at[-2:-1], placed)
        rest, placed = lax.optimization_barrier((far[:-1], placed))
        swapped = [swap(x) for x in rest]
        placed = _place(source, rest + [first], at[2:-2:2] + at[-1:], placed)
        cosine, affinity = _tiles(counts, source, swapped, at[3:-1:2], placed)
        return cosine[:, None], affinity[:, None]

    placed = (
        P("docs", "feat"),
        P("docs", "feat"),
        P("feat", None),
        P("docs", "feat", None),
        P("docs", "feat"),
    )
    return jax.shard_map(
        per_device,
        mesh=mesh,
        in_specs=placed,
        out_specs=(P("docs", "feat", None, None), P("docs", "feat", None)),
        check_vma=False,
    )
```
